32 devices in a mesh: az: 16 (over z, y, core), rad: 2 (over x).
Axes of the slice: x: 2, y: 2, z: 4, core: 2. Of those that a mesh axis runs over, the one named last changes fastest.
Arguments:
- density: float32 [256, 96, 128], P('az', 'rad'), may hold values from 0.5 to 1.5
- flow_vars: float32 [4, 256, 96, 128], P(None, 'az', 'rad'), may hold values from -6 to 6
- blade_offset: int32 [4], replicated, may hold values from 0 to 4, as said below
- smooth_width: int32 [128], replicated, may hold values from 1 to 4, as said below
Outputs:
- mean_fields: float32 [5, 256, 96, 128], P(None, 'az', 'rad')
- q_field: float32 [256, 96, 128], P('az', 'rad')
The draws below stay inside these ranges and needn't reach their ends.
Inputs may be any that keep to these rules, and one draw needn't show every extreme that they name: `blade_offset`: some blade's passage has the offset 4. `smooth_width`: some axial station uses the half-width 4.
All inputs are finite; a program needn't handle non-finite values.
Results may differ from the reference program's by a relative error of at most 0.00002.
Values sent between devices are 32-bit elements; how exact they have to be, the bound alone decides.
A program may use at most 64 MiB of HBM per device.

```python
import math
import jax
import jax.numpy as jnp
from jax import lax

Z = 128
BLADES = 4
MAXOFF = 4
HW = 4
AZ = 256
R = 96


def draw_blade_offset(key, part):
    base_key = jax.random.fold_in(key, 11)
    value_key, choose_key = jax.random.split(base_key)
    values = jax.random.randint(value_key, (BLADES,), 0, MAXOFF + 1, dtype=jnp.int32)
    chosen = jax.random.randint(choose_key, (), 0, BLADES, dtype=jnp.int32)
    return jnp.where(jnp.arange(BLADES, dtype=jnp.int32) == chosen, MAXOFF, values).astype(jnp.int32)


def draw_smooth_width(key, part):
    base_key = jax.random.fold_in(key, 23)
    value_key, choose_key = jax.random.split(base_key)
    values = jax.random.randint(value_key, (Z,), 1, HW + 1, dtype=jnp.int32)
    chosen = jax.random.randint(choose_key, (), 0, Z, dtype=jnp.int32)
    return jnp.where(jnp.arange(Z, dtype=jnp.int32) == chosen, HW, values).astype(jnp.int32)


def steps_of(rng, shape, pieces, low, high):
    def one(dim, parts):
        steps = jax.random.uniform(jax.random.fold_in(jax.random.fold_in(rng, 6), dim), (parts,), jnp.float32, low / len(pieces), high / len(pieces))
        return jnp.repeat(jnp.exp(steps), shape[dim] // parts).reshape((-1,) + (1,) * (len(shape) - dim - 1))

    level = one(*pieces[0])
    for cut in pieces[1:]:
        level = level * one(*cut)
    return level


def gaussian(key, dims, scale, reach, cuts=(), kind=jnp.bfloat16):
    result = jax.random.normal(key, dims, jnp.float32) * scale
    if len(cuts) > 0:
        result = steps_of(key, dims, cuts, -0.22, 0.18) * result
    return jnp.clip(result, min=-reach, max=reach).astype(kind)


def setup_inputs(seed: int = 0) -> dict:
    arg_keys = jax.random.split(jax.random.key(seed), 5)
    density = jnp.clip(0.5 + 1.0 * jax.random.uniform(arg_keys[0], (AZ, R, Z), jnp.float32) ** steps_of(arg_keys[0], (AZ, R, Z), ((0, 16), (1, 2)), -0.2, 0.2), 0.5, 1.5)
    flow_vars = gaussian(arg_keys[1], (4, AZ, R, Z), 1.0, 6.0, ((1, 16), (2, 2)), jnp.float32)
    blade_offset = draw_blade_offset(jax.random.fold_in(arg_keys[4], 71), 0)
    smooth_width = draw_smooth_width(jax.random.fold_in(arg_keys[4], 71), 0)
    return dict(density=density, flow_vars=flow_vars, blade_offset=blade_offset, smooth_width=smooth_width)


def smoothing_taps(smooth_width):
    spread = jnp.arange(-HW, HW + 1)
    width = smooth_width.astype(jnp.float32)
    square = (spread.astype(jnp.float32) ** 2)[:, None]
    weights = jnp.where(jnp.abs(spread)[:, None] <= smooth_width[None, :], jnp.exp(-0.5 * square / (width * width)[None, :]), 0.0)
    return weights / jnp.sum(weights, axis=0, keepdims=True)


def edge_rate(field, axis):
    count = field.shape[axis]
    upper = jnp.concatenate([lax.slice_in_dim(field, 1, count, axis=axis), lax.slice_in_dim(field, count - 1, count, axis=axis)], axis=axis)
    lower = jnp.concatenate([lax.slice_in_dim(field, 0, 1, axis=axis), lax.slice_in_dim(field, 0, count - 1, axis=axis)], axis=axis)
    places = jnp.arange(count)
    span = jnp.where((places == 0) | (places == count - 1), 1.0, 2.0).astype(field.dtype)
    layout = [1] * field.ndim
    layout[axis] = count
    return (upper - lower) / span.reshape(layout)


def swirl_measure(smoothed, az_rate, radial_rate, axial_rate, radius):
    tensor_aa = radial_rate[0]
    tensor_ab = (az_rate[0] - smoothed[1]) / radius
    tensor_ac = axial_rate[0]
    tensor_ba = radial_rate[1]
    tensor_bb = (az_rate[1] + smoothed[0]) / radius
    tensor_bc = axial_rate[1]
    tensor_ca = radial_rate[2]
    tensor_cb = az_rate[2] / radius
    tensor_cc = axial_rate[2]
    diagonal_part = tensor_aa * tensor_aa + tensor_bb * tensor_bb + tensor_cc * tensor_cc
    cross_part = tensor_ab * tensor_ba + tensor_ac * tensor_ca + tensor_bc * tensor_cb
    return -0.5 * (diagonal_part + 2.0 * cross_part)


def reference(density, flow_vars, blade_offset, smooth_width):
    velocity = flow_vars[0:3]
    carried = jnp.concatenate([density[None], density[None] * velocity, flow_vars[3:4]], axis=0)
    sector = AZ // BLADES
    phase = jnp.arange(sector).astype(jnp.int32)
    sector_sums = jnp.zeros((5, sector, R, Z), jnp.float32)
    for blade in range(BLADES):
        index = ((blade * sector + blade_offset[blade] + phase) % AZ).astype(jnp.int32)
        sector_sums = sector_sums + jnp.take(carried, index, axis=1)
    theta = jnp.arange(AZ).astype(jnp.int32)
    owner = (theta // sector).astype(jnp.int32)
    table_offset = jnp.take(blade_offset, owner)
    local_phase = ((theta % sector - table_offset) % sector).astype(jnp.int32)
    phase_sums = jnp.take(sector_sums, local_phase, axis=1)
    mean_fields = jnp.concatenate([phase_sums[0:1] / BLADES, phase_sums[1:4] / phase_sums[0:1], phase_sums[4:5] / BLADES], axis=0)
    fluctuation = velocity - mean_fields[1:4]
    taps = smoothing_taps(smooth_width)
    smoothed = jnp.zeros_like(fluctuation)
    for turn in range(2 * HW + 1):
        smoothed = smoothed + taps[turn] * jnp.roll(fluctuation, HW - turn, axis=1)
    dtheta = 2.0 * math.pi / AZ
    az_rate = (jnp.roll(smoothed, -1, axis=1) - jnp.roll(smoothed, 1, axis=1)) / (2.0 * dtheta)
    radial_rate = edge_rate(smoothed, 2)
    axial_rate = edge_rate(smoothed, 3)
    radius = (R / 2 + jnp.arange(R).astype(jnp.float32) + 0.5)[:, None]
    q_field = swirl_measure(smoothed, az_rate, radial_rate, axial_rate, radius)
    return mean_fields, q_field
```

```python
import functools
import math

import jax
import jax.numpy as jnp
from jax import lax
from jax.experimental import pallas as pl
from jax.experimental.pallas import tpu as pltpu
from jax.sharding import PartitionSpec as P

BLADES = 4
MAXOFF = 4
HW = 4
ROWS = 8
PAIR = 2
SKEW = 2
LAG = 1
RIM = HW + 1
BACK = RIM + MAXOFF
MESH = pl.DeviceIdType.MESH


def kernel(
    n_az,
    n_rad,
    off_ref,
    width_ref,
    density,
    flow,
    mean_out,
    q_out,
    ahead,
    vprev,
    vnext,
    cbuf,
    precv,
    psend,
    srecv,
    ssend,
    text,
    stage,
    fl,
    sm,
    edge_s,
    edge_r,
    taps,
    ahead_sem,
    v_sem,
    up_sem,
    down_sem,
    next_sem,
    prev_sem,
    edge_sem,
):
    cells, rad_cells = density.shape[0], density.shape[1]
    blocks = rad_cells // ROWS
    main = 4 * blocks // PAIR
    per_block = 4 // PAIR
    chunks = 5 * blocks // PAIR
    group = n_az // BLADES
    place = lax.axis_index("az")
    rad = lax.axis_index("rad")
    blade = place // group
    local = place % group
    first = blade * group
    ring_next = first + (local + 1) % group
    ring_prev = first + (local + group - 1) % group
    cyc_next = (place + 1) % n_az
    cyc_prev = (place + n_az - 1) % n_az
    has_up, has_down = blade < BLADES - 1, blade > 0
    has_out, has_in = rad < n_rad - 1, rad > 0
    up, down = place + group, place - group

    off_own = off_ref[blade]
    off_before = off_ref[(blade + BLADES - 1) % BLADES]
    off_after = off_ref[(blade + 1) % BLADES]
    off_tail = jnp.where(local == group - 1, off_before, off_own)
    off_low = jnp.where(local == 0, off_before, off_own)
    off_high = jnp.where(local == group - 1, off_after, off_own)

    def phys(k):
        return jnp.where(rad % 2 == 0, blocks - 1 - k, k)

    def radial(k):
        return pl.ds(pl.multiple_of(phys(k) * ROWS, ROWS), ROWS)

    def remote(src, dst, sems, index, az=None, to_rad=None):
        device = {"az": place if az is None else az, "rad": rad if to_rad is None else to_rad}
        return pltpu.make_async_remote_copy(
            src_ref=src,
            dst_ref=dst,
            send_sem=sems.at[0, index],
            recv_sem=sems.at[1, index],
            device_id=device,
            device_id_type=MESH,
        )

    def ahead_density(k):
        return remote(
            density.at[pl.ds(0, MAXOFF), radial(k)], ahead.at[k, 0], ahead_sem, 2 * k, az=ring_prev
        )

    def ahead_flow(k):
        return remote(
            flow.at[:, pl.ds(0, MAXOFF), radial(k)],
            ahead.at[k, pl.ds(1, 4)],
            ahead_sem,
            2 * k + 1,
            az=ring_prev,
        )

    def rim_next():
        return remote(flow.at[pl.ds(0, 3), pl.ds(cells - RIM, RIM)], vprev, v_sem, 0, az=cyc_next)

    def rim_prev():
        return remote(flow.at[pl.ds(0, 3), pl.ds(0, RIM)], vnext, v_sem, 1, az=cyc_prev)

    def slots(c):
        return pl.ds(c * PAIR, PAIR)

    def send_up(src, c):
        return remote(src.at[slots(c)], precv.at[slots(c)], up_sem, c, az=up)

    def send_down(src, c):
        return remote(src.at[slots(c)], srecv.at[slots(c)], down_sem, c, az=down)

    def sums_next(k):
        four = pl.ds(4 * k, 4)
        return remote(
            text.at[four, pl.ds(cells, BACK)], text.at[four, pl.ds(0, BACK)], next_sem, k, az=ring_next
        )

    def sums_prev(k):
        four = pl.ds(4 * k, 4)
        return remote(
            text.at[four, pl.ds(BACK, RIM)],
            text.at[four, pl.ds(BACK + cells, RIM)],
            prev_sem,
            k,
            az=ring_prev,
        )

    def pressure_next(c):
        return remote(
            text.at[slots(c), pl.ds(BACK + cells - MAXOFF, MAXOFF)],
            text.at[slots(c), pl.ds(BACK - MAXOFF, MAXOFF)],
            next_sem,
            blocks + c - main,
            az=ring_next,
        )

    def edge(side):
        return remote(
            edge_s.at[side], edge_r.at[side], edge_sem, side, to_rad=rad + 1 if side else rad - 1
        )

    barrier = pltpu.get_barrier_semaphore()

    def greet(az=None, to_rad=None):
        pl.semaphore_signal(
            barrier,
            inc=1,
            device_id={"az": place if az is None else az, "rad": rad if to_rad is None else to_rad},
            device_id_type=MESH,
        )

    for other in (ring_next, ring_prev, cyc_next, cyc_prev):
        greet(az=other)
    pl.when(has_up)(lambda: greet(az=up))
    pl.when(has_down)(lambda: greet(az=down))
    pl.when(has_out)(lambda: greet(to_rad=rad + 1))
    pl.when(has_in)(lambda: greet(to_rad=rad - 1))

    width = width_ref[...].astype(jnp.float32)
    weights = [
        jnp.where(m <= width_ref[...], jnp.exp((-0.5 * m * m) / (width * width)), 0.0)
        for m in range(HW + 1)
    ]
    whole = weights[0] + 2.0 * sum(weights[1:])
    for m in range(HW + 1):
        taps[m] = jnp.broadcast_to(weights[m] / whole, (ROWS, width.shape[1]))

    greeted = 4
    for flag in (has_up, has_down, has_out, has_in):
        greeted = greeted + jnp.where(flag, 1, 0)
    pl.semaphore_wait(barrier, greeted)

    @pl.loop(0, blocks)
    def _(k):
        ahead_density(k).start()
        ahead_flow(k).start()

    rim_next().start()
    rim_prev().start()

    def make_carried(k):
        ahead_density(k).wait_recv()
        ahead_flow(k).wait_recv()
        js = radial(k)
        sure = cells - MAXOFF
        rho = density[pl.ds(off_own, sure), js, :]
        cbuf[4 * k, 0:sure] = rho
        for c in range(3):
            cbuf[4 * k + 1 + c, 0:sure] = rho * flow[c, pl.ds(off_own, sure), js, :]
        cbuf[4 * blocks + k, 0:sure] = flow[3, pl.ds(off_own, sure), js, :]
        for i in range(sure, cells):
            row = jnp.minimum(i + off_own, cells - 1)
            mine = jnp.where(i + off_own < cells, 1.0, 0.0)
            rho = density[row, js, :] * mine
            total = [rho] + [rho * flow[c, row, js, :] for c in range(3)]
            total.append(flow[3, row, js, :] * mine)
            for j in range(i - sure + 1):
                theirs = jnp.where(i + off_tail == cells + j, 1.0, 0.0)
                rho = ahead[k, 0, j] * theirs
                terms = [rho] + [rho * ahead[k, 1 + c, j] for c in range(3)]
                terms.append(ahead[k, 4, j] * theirs)
                total = [a + b for a, b in zip(total, terms)]
            for f in range(4):
                cbuf[4 * k + f, i] = total[f]
            cbuf[4 * blocks + k, i] = total[4]

    def go_up(c):
        @pl.when(jnp.logical_not(has_down))
        def _():
            send_up(cbuf, c).start()

        @pl.when(has_down)
        def _():
            send_up(psend, c).wait_recv()

            @pl.when(has_up)
            def _():
                psend[slots(c)] = precv[slots(c)] + cbuf[slots(c)]
                send_up(psend, c).start()

    def go_down(c):
        @pl.when(jnp.logical_not(has_up))
        def _():
            send_down(cbuf, c).start()

        @pl.when(has_up)
        def _():
            send_down(ssend, c).wait_recv()

            @pl.when(has_down)
            def _():
                ssend[slots(c)] = srecv[slots(c)] + cbuf[slots(c)]
                send_down(ssend, c).start()

    def finish(c):
        own = pl.ds(BACK, cells)

        @pl.when(jnp.logical_not(has_down))
        def _():
            text[slots(c), own] = cbuf[slots(c)] + srecv[slots(c)]

        @pl.when(jnp.logical_not(has_up))
        def _():
            text[slots(c), own] = cbuf[slots(c)] + precv[slots(c)]

        @pl.when(jnp.logical_and(has_up, has_down))
        def _():
            text[slots(c), own] = psend[slots(c)] + srecv[slots(c)]

        @pl.when(jnp.logical_and(c < main, c % per_block == per_block - 1))
        def _():
            sums_next(c // per_block).start()
            sums_prev(c // per_block).start()

        @pl.when(c >= main)
        def _():
            pressure_next(c).start()

    def smooth_block(k):
        sums_next(k).wait_recv()
        sums_prev(k).wait_recv()
        js = radial(k)
        for f in range(4):
            stage[f] = text[4 * k + f]
        for at, count, off, source, row in (
            (0, RIM, off_low, vprev, 0),
            (RIM, cells, off_own, flow, 0),
            (RIM + cells, RIM, off_high, vnext, 0),
        ):
            rows = pl.ds(at + MAXOFF - off, count)
            rho = stage[0, rows]
            inverse = 1.0 / rho
            if source is flow:
                mean_out[0, :, js, :] = rho * (1.0 / BLADES)
            for c in range(3):
                mean = stage[1 + c, rows] * inverse
                if source is flow:
                    mean_out[1 + c, :, js, :] = mean
                fl[c, at : at + count] = source[c, :, js, :] - mean
        span = cells + 2
        js = pl.ds(pl.multiple_of(ROWS + phys(k) * ROWS, ROWS), ROWS)
        for c in range(3):
            total = taps[0] * fl[c, HW : HW + span]
            for m in range(1, HW + 1):
                total = total + taps[m] * (
                    fl[c, HW - m : HW - m + span] + fl[c, HW + m : HW + m + span]
                )
            sm[c, :, js, :] = total

        @pl.when(jnp.logical_and(has_out, phys(k) == blocks - 1))
        def _():
            for c in range(3):
                edge_s[1, c] = sm[c, 1 : cells + 1, ROWS + rad_cells - 1, :]
            edge(1).start()

        @pl.when(jnp.logical_and(has_in, phys(k) == 0))
        def _():
            for c in range(3):
                edge_s[0, c] = sm[c, 1 : cells + 1, ROWS, :]
            edge(0).start()

    def swirl():
        mid = slice(1, cells + 1)
        for side, have, at, own in (
            (0, has_out, ROWS + rad_cells, ROWS + rad_cells - 1),
            (1, has_in, ROWS - 1, ROWS),
        ):

            @pl.when(have)
            def _():
                edge(side).wait_recv()
                for c in range(3):
                    sm[c, mid, at, :] = edge_r[side, c]

            @pl.when(jnp.logical_not(have))
            def _():
                for c in range(3):
                    sm[c, mid, at, :] = sm[c, mid, own, :]

        shape = (ROWS, density.shape[2])
        lanes = shape[1]
        lane = lax.broadcasted_iota(jnp.int32, shape, 1)
        line = lax.broadcasted_iota(jnp.int32, shape, 0)
        is_end = lane == lanes - 1
        is_start = lane == 0
        axial_scale = jnp.where(jnp.logical_or(is_end, is_start), 1.0, 0.5)
        az_scale = n_az * cells / (4.0 * math.pi)
        for b in range(blocks):
            rows = rad * rad_cells + b * ROWS + line
            ends = jnp.logical_or(rows == 0, rows == n_rad * rad_cells - 1)
            radial_scale = jnp.where(ends, 1.0, 0.5)
            inv_radius = 1.0 / (n_rad * rad_cells / 2 + rows.astype(jnp.float32) + 0.5)
            low = ROWS * (b + 1)

            def row_of(i, carry):
                here = [sm[c, i + 1, low : low + ROWS, :] for c in range(3)]
                rr, ar, xr = [], [], []
                for c in range(3):
                    above = sm[c, i + 1, low + 1 : low + 1 + ROWS, :]
                    below = sm[c, i + 1, low - 1 : low - 1 + ROWS, :]
                    rr.append((above - below) * radial_scale)
                    later = sm[c, i + 2, low : low + ROWS, :]
                    sooner = sm[c, i, low : low + ROWS, :]
                    ar.append((later - sooner) * az_scale)
                    right = jnp.where(is_end, here[c], pltpu.roll(here[c], lanes - 1, 1))
                    left = jnp.where(is_start, here[c], pltpu.roll(here[c], 1, 1))
                    xr.append((right - left) * axial_scale)
                ab = (ar[0] - here[1]) * inv_radius
                bb = (ar[1] + here[0]) * inv_radius
                cb = ar[2] * inv_radius
                diagonal = rr[0] * rr[0] + bb * bb + xr[2] * xr[2]
                cross = ab * rr[1] + xr[0] * rr[2] + xr[1] * cb
                q_out[i, b * ROWS : (b + 1) * ROWS, :] = -0.5 * (diagonal + 2.0 * cross)
                return carry

            lax.fori_loop(0, cells, row_of, 0, unroll=2)

    def put_pressure(c):
        pressure_next(c).wait_recv()
        for e in range(PAIR):
            stage[e] = text[c * PAIR + e]
            k = (c - main) * PAIR + e
            mean_out[4, :, radial(k), :] = stage[e, pl.ds(BACK - off_own, cells)] * (1.0 / BLADES)

    hops = BLADES - 1

    @pl.loop(0, chunks + SKEW * hops + LAG)
    def _(s):
        @pl.when(jnp.logical_and(s < main, s % per_block == 0))
        def _():
            make_carried(s // per_block)

        u = s - SKEW * blade
        pl.when(jnp.logical_and(u >= 0, u < chunks))(lambda: go_up(u))
        w = s - SKEW * (hops - blade)
        pl.when(jnp.logical_and(w >= 0, w < chunks))(lambda: go_down(w))
        t = s - SKEW * hops
        pl.when(jnp.logical_and(t >= 0, t < chunks))(lambda: finish(t))
        g = t - LAG

        @pl.when(g == per_block - 1)
        def _():
            rim_next().wait_recv()
            rim_prev().wait_recv()

        @pl.when(jnp.logical_and(jnp.logical_and(g >= 0, g < main), g % per_block == per_block - 1))
        def _():
            smooth_block(g // per_block)

        pl.when(g == main - 1)(swirl)
        pl.when(g >= main)(lambda: put_pressure(g))

    @pl.loop(0, blocks)
    def _(k):
        ahead_density(k).wait_send()
        ahead_flow(k).wait_send()
        sums_next(k).wait_send()
        sums_prev(k).wait_send()

    @pl.loop(0, chunks)
    def _(c):
        pl.when(has_up)(lambda: send_up(psend, c).wait_send())
        pl.when(has_down)(lambda: send_down(ssend, c).wait_send())
        pl.when(c >= main)(lambda: pressure_next(c).wait_send())

    rim_next().wait_send()
    rim_prev().wait_send()
    pl.when(has_out)(lambda: edge(1).wait_send())
    pl.when(has_in)(lambda: edge(0).wait_send())


def shards(n_az, n_rad, density, flow_vars, blade_offset, smooth_width):
    cells, rad_cells, axial = density.shape
    blocks = rad_cells // ROWS
    count = 5 * blocks
    chunks = count // PAIR
    f32 = jnp.float32
    vmem = pl.BlockSpec(memory_space=pltpu.VMEM)
    block = (count, cells, ROWS, axial)
    dma = pltpu.SemaphoreType.DMA
    return pl.pallas_call(
        functools.partial(kernel, n_az, n_rad),
        out_shape=(
            jax.ShapeDtypeStruct((5, cells, rad_cells, axial), f32),
            jax.ShapeDtypeStruct((cells, rad_cells, axial), f32),
        ),
        in_specs=[pl.BlockSpec(memory_space=pltpu.SMEM), vmem, vmem, vmem],
        out_specs=(vmem, vmem),
        scratch_shapes=[
            pltpu.VMEM((blocks, 5, MAXOFF, ROWS, axial), f32),
            pltpu.VMEM((3, RIM, rad_cells, axial), f32),
            pltpu.VMEM((3, RIM, rad_cells, axial), f32),
            pltpu.VMEM(block, f32),
            pltpu.VMEM(block, f32),
            pltpu.VMEM(block, f32),
            pltpu.VMEM(block, f32),
            pltpu.VMEM(block, f32),
            pltpu.VMEM((count, BACK + cells + RIM, ROWS, axial), f32),
            pltpu.VMEM((4, BACK + cells + RIM, ROWS, axial), f32),
            pltpu.VMEM((3, cells + 2 * RIM, ROWS, axial), f32),
            pltpu.VMEM((3, cells + 2, rad_cells + 2 * ROWS, axial), f32),
            pltpu.VMEM((2, 3, cells, axial), f32),
            pltpu.VMEM((2, 3, cells, axial), f32),
            pltpu.VMEM((HW + 1, ROWS, axial), f32),
            dma((2, 2 * blocks)),
            dma((2, 2)),
            dma((2, chunks)),
            dma((2, chunks)),
            dma((2, blocks + blocks // PAIR)),
            dma((2, blocks)),
            dma((2, 2)),
        ],
        compiler_params=pltpu.CompilerParams(
            collective_id=0, has_side_effects=True, vmem_limit_bytes=48 * 1024 * 1024
        ),
    )(blade_offset, smooth_width.reshape(1, axial), density, flow_vars)


def solution(mesh):
    in_specs = (P("az", "rad", None), P(None, "az", "rad", None), P(), P())
    out_specs = (P(None, "az", "rad", None), P("az", "rad", None))
    body = functools.partial(shards, mesh.shape["az"], mesh.shape["rad"])
    return jax.shard_map(body, mesh=mesh, in_specs=in_specs, out_specs=out_specs, check_vma=False)
```

```python
import functools
import math

import jax
import jax.numpy as jnp
from jax import lax
from jax.experimental import pallas as pl
from jax.experimental.pallas import tpu as pltpu
from jax.sharding import PartitionSpec as P

BLADES = 4
MAXOFF = 4
HW = 4
ROWS = 8
SPLIT = 4
SKEW = 4
LAG = 8
RIM = HW + 1
BACK = RIM + MAXOFF
MESH = pl.DeviceIdType.MESH


def kernel(
    n_az,
    n_rad,
    off_hbm,
    width_hbm,
    density_hbm,
    flow_hbm,
    mean_out,
    q_out,
    off_ref,
    width_ref,
    density,
    flow,
    ahead,
    vprev,
    vnext,
    cbuf,
    precv,
    psend,
    srecv,
    ssend,
    text,
    stage,
    fl,
    sm,
    edge_s,
    edge_r,
    taps,
    ahead_sem,
    v_sem,
    up_sem,
    down_sem,
    next_sem,
    prev_sem,
    edge_sem,
    load_sem,
):
    cells, rad_cells = density.shape[0], density.shape[1]
    blocks = rad_cells // ROWS
    main = SPLIT * blocks
    chunks = main + main // 4
    part = cells // SPLIT
    joint = 4 // SPLIT
    group = n_az // BLADES
    place = lax.axis_index("az")
    rad = lax.axis_index("rad")
    blade = place // group
    local = place % group
    first = blade * group
    ring_next = first + (local + 1) % group
    ring_prev = first + (local + group - 1) % group
    cyc_next = (place + 1) % n_az
    cyc_prev = (place + n_az - 1) % n_az
    has_up, has_down = blade < BLADES - 1, blade > 0
    has_out, has_in = rad < n_rad - 1, rad > 0
    up, down = place + group, place - group

    loads = [
        pltpu.make_async_copy(src, dst, load_sem.at[i])
        for i, (src, dst) in enumerate(
            (
                (off_hbm, off_ref),
                (width_hbm, width_ref),
                (density_hbm, density),
                (flow_hbm, flow),
            )
        )
    ]
    for load in loads:
        load.start()

    barrier = pltpu.get_barrier_semaphore()

    def greet(az=None, to_rad=None):
        pl.semaphore_signal(
            barrier,
            inc=1,
            device_id={"az": place if az is None else az, "rad": rad if to_rad is None else to_rad},
            device_id_type=MESH,
        )

    for other in (ring_next, ring_prev, cyc_next, cyc_prev):
        greet(az=other)
    pl.when(has_up)(lambda: greet(az=up))
    pl.when(has_down)(lambda: greet(az=down))
    pl.when(has_out)(lambda: greet(to_rad=rad + 1))
    pl.when(has_in)(lambda: greet(to_rad=rad - 1))

    for load in loads:
        load.wait()

    off_own = off_ref[blade]
    off_before = off_ref[(blade + BLADES - 1) % BLADES]
    off_after = off_ref[(blade + 1) % BLADES]
    off_tail = jnp.where(local == group - 1, off_before, off_own)
    off_low = jnp.where(local == 0, off_before, off_own)
    off_high = jnp.where(local == group - 1, off_after, off_own)

    def phys(k):
        return jnp.where(rad % 2 == 0, blocks - 1 - k, k)

    def radial(k):
        return pl.ds(pl.multiple_of(phys(k) * ROWS, ROWS), ROWS)

    def remote(src, dst, sems, index, az=None, to_rad=None):
        device = {"az": place if az is None else az, "rad": rad if to_rad is None else to_rad}
        return pltpu.make_async_remote_copy(
            src_ref=src,
            dst_ref=dst,
            send_sem=sems.at[0, index],
            recv_sem=sems.at[1, index],
            device_id=device,
            device_id_type=MESH,
        )

    def ahead_density(k):
        return remote(
            density.at[pl.ds(0, MAXOFF), radial(k)], ahead.at[k, 0], ahead_sem, 2 * k, az=ring_prev
        )

    def ahead_flow(k):
        return remote(
            flow.at[:, pl.ds(0, MAXOFF), radial(k)],
            ahead.at[k, pl.ds(1, 4)],
            ahead_sem,
            2 * k + 1,
            az=ring_prev,
        )

    def rim_next(k):
        rows = flow.at[pl.ds(0, 3), pl.ds(cells - RIM, RIM), radial(k)]
        return remote(rows, vprev.at[k], v_sem, 2 * k, az=cyc_next)

    def rim_prev(k):
        rows = flow.at[pl.ds(0, 3), pl.ds(0, RIM), radial(k)]
        return remote(rows, vnext.at[k], v_sem, 2 * k + 1, az=cyc_prev)

    def send_up(src, c):
        return remote(src.at[c], precv.at[c], up_sem, c, az=up)

    def send_down(src, c):
        return remote(src.at[c], srecv.at[c], down_sem, c, az=down)

    def sums_next(k):
        four = pl.ds(4 * k, 4)
        return remote(
            text.at[four, pl.ds(cells, BACK)], text.at[four, pl.ds(0, BACK)], next_sem, k, az=ring_next
        )

    def sums_prev(k):
        four = pl.ds(4 * k, 4)
        return remote(
            text.at[four, pl.ds(BACK, RIM)],
            text.at[four, pl.ds(BACK + cells, RIM)],
            prev_sem,
            k,
            az=ring_prev,
        )

    def pressure_next(c):
        these = pl.ds(4 * blocks + (c - main) * joint, joint)
        return remote(
            text.at[these, pl.ds(BACK + cells - MAXOFF, MAXOFF)],
            text.at[these, pl.ds(BACK - MAXOFF, MAXOFF)],
            next_sem,
            blocks + c - main,
            az=ring_next,
        )

    def edge(side):
        return remote(
            edge_s.at[side], edge_r.at[side], edge_sem, side, to_rad=rad + 1 if side else rad - 1
        )

    width = width_ref[...].astype(jnp.float32)
    weights = [
        jnp.where(m <= width_ref[...], jnp.exp((-0.5 * m * m) / (width * width)), 0.0)
        for m in range(HW + 1)
    ]
    whole = weights[0] + 2.0 * sum(weights[1:])
    for m in range(HW + 1):
        taps[m] = jnp.broadcast_to(weights[m] / whole, (ROWS, width.shape[1]))

    greeted = 4
    for flag in (has_up, has_down, has_out, has_in):
        greeted = greeted + jnp.where(flag, 1, 0)
    pl.semaphore_wait(barrier, greeted)

    ahead_density(0).start()
    ahead_flow(0).start()
    sure = cells - MAXOFF

    def pressure_at(k, i):
        unit = SPLIT * k + i // part
        return main + unit // 4, unit % 4

    def make_carried(k):
        js = radial(k)
        for low in range(0, sure, part):
            n = min(part, sure - low)
            rows = pl.ds(off_own + low, n)
            chunk = SPLIT * k + low // part
            rho = density[rows, js, :]
            cbuf[chunk, 0, 0:n] = rho
            for c in range(3):
                cbuf[chunk, 1 + c, 0:n] = rho * flow[c, rows, js, :]
            at, unit = pressure_at(k, low)
            cbuf[at, unit, 0:n] = flow[3, rows, js, :]

    def make_tail(k):
        ahead_density(k).wait_recv()
        ahead_flow(k).wait_recv()
        js = radial(k)
        for i in range(sure, cells):
            row = jnp.minimum(i + off_own, cells - 1)
            mine = jnp.where(i + off_own < cells, 1.0, 0.0)
            rho = density[row, js, :] * mine
            total = [rho] + [rho * flow[c, row, js, :] for c in range(3)]
            total.append(flow[3, row, js, :] * mine)
            for j in range(i - sure + 1):
                theirs = jnp.where(i + off_tail == cells + j, 1.0, 0.0)
                rho = ahead[k, 0, j] * theirs
                terms = [rho] + [rho * ahead[k, 1 + c, j] for c in range(3)]
                terms.append(ahead[k, 4, j] * theirs)
                total = [a + b for a, b in zip(total, terms)]
            for f in range(4):
                cbuf[SPLIT * k + i // part, f, i % part] = total[f]
            at, unit = pressure_at(k, i)
            cbuf[at, unit, i % part] = total[4]

    def go_up(c):
        @pl.when(jnp.logical_not(has_down))
        def _():
            send_up(cbuf, c).start()

        @pl.when(has_down)
        def _():
            send_up(psend, c).wait_recv()

            @pl.when(has_up)
            def _():
                psend[c] = precv[c] + cbuf[c]
                send_up(psend, c).start()

    def go_down(c):
        @pl.when(jnp.logical_not(has_up))
        def _():
            send_down(cbuf, c).start()

        @pl.when(has_up)
        def _():
            send_down(ssend, c).wait_recv()

            @pl.when(has_down)
            def _():
                ssend[c] = srecv[c] + cbuf[c]
                send_down(ssend, c).start()

    def place_sums(c, left, right):
        @pl.when(c < main)
        def _():
            rows = pl.ds(BACK + (c % SPLIT) * part, part)
            text[pl.ds(4 * (c // SPLIT), 4), rows] = left[c] + right[c]

        @pl.when(c >= main)
        def _():
            for e in range(4):
                slot = 4 * blocks + (c - main) * joint + e // SPLIT
                low = BACK + (e % SPLIT) * part
                text[slot, low : low + part] = left[c, e] + right[c, e]

    def finish(c):
        pl.when(jnp.logical_not(has_down))(lambda: place_sums(c, cbuf, srecv))
        pl.when(jnp.logical_not(has_up))(lambda: place_sums(c, cbuf, precv))
        pl.when(jnp.logical_and(has_up, has_down))(lambda: place_sums(c, psend, srecv))

        @pl.when(jnp.logical_and(c < main, c % SPLIT == SPLIT - 1))
        def _():
            sums_next(c // SPLIT).start()
            sums_prev(c // SPLIT).start()

        @pl.when(c >= main)
        def _():
            pressure_next(c).start()

    def smooth_block(k):
        sums_next(k).wait_recv()
        sums_prev(k).wait_recv()
        rim_next(k).wait_recv()
        rim_prev(k).wait_recv()
        js = radial(k)
        for f in range(4):
            stage[f] = text[4 * k + f]
        for at, count, off, source in (
            (0, RIM, off_low, vprev),
            (RIM, cells, off_own, flow),
            (RIM + cells, RIM, off_high, vnext),
        ):
            rows = pl.ds(at + MAXOFF - off, count)
            rho = stage[0, rows]
            inverse = 1.0 / rho
            if source is flow:
                mean_out[0, :, js, :] = rho * (1.0 / BLADES)
            for c in range(3):
                mean = stage[1 + c, rows] * inverse
                if source is flow:
                    mean_out[1 + c, :, js, :] = mean
                here = source[c, :, js, :] if source is flow else source[k, c]
                fl[c, at : at + count] = here - mean
        span = cells + 2
        js = pl.ds(pl.multiple_of(ROWS + phys(k) * ROWS, ROWS), ROWS)
        for c in range(3):
            total = taps[0] * fl[c, HW : HW + span]
            for m in range(1, HW + 1):
                total = total + taps[m] * (
                    fl[c, HW - m : HW - m + span] + fl[c, HW + m : HW + m + span]
                )
            sm[c, :, js, :] = total

        @pl.when(jnp.logical_and(has_out, phys(k) == blocks - 1))
        def _():
            for c in range(3):
                edge_s[1, c] = sm[c, 1 : cells + 1, ROWS + rad_cells - 1, :]
            edge(1).start()

        @pl.when(jnp.logical_and(has_in, phys(k) == 0))
        def _():
            for c in range(3):
                edge_s[0, c] = sm[c, 1 : cells + 1, ROWS, :]
            edge(0).start()

    def swirl():
        mid = slice(1, cells + 1)
        for side, have, at, own in (
            (0, has_out, ROWS + rad_cells, ROWS + rad_cells - 1),
            (1, has_in, ROWS - 1, ROWS),
        ):

            @pl.when(have)
            def _():
                edge(side).wait_recv()
                for c in range(3):
                    sm[c, mid, at, :] = edge_r[side, c]

            @pl.when(jnp.logical_not(have))
            def _():
                for c in range(3):
                    sm[c, mid, at, :] = sm[c, mid, own, :]

        shape = (ROWS, density.shape[2])
        lanes = shape[1]
        lane = lax.broadcasted_iota(jnp.int32, shape, 1)
        line = lax.broadcasted_iota(jnp.int32, shape, 0)
        is_end = lane == lanes - 1
        is_start = lane == 0
        axial_scale = jnp.where(jnp.logical_or(is_end, is_start), 1.0, 0.5)
        az_scale = n_az * cells / (4.0 * math.pi)
        for b in range(blocks):
            rows = rad * rad_cells + b * ROWS + line
            ends = jnp.logical_or(rows == 0, rows == n_rad * rad_cells - 1)
            radial_scale = jnp.where(ends, 1.0, 0.5)
            inv_radius = 1.0 / (n_rad * rad_cells / 2 + rows.astype(jnp.float32) + 0.5)
            low = ROWS * (b + 1)

            def row_of(i, carry):
                here = [sm[c, i + 1, low : low + ROWS, :] for c in range(3)]
                rr, ar, xr = [], [], []
                for c in range(3):
                    above = sm[c, i + 1, low + 1 : low + 1 + ROWS, :]
                    below = sm[c, i + 1, low - 1 : low - 1 + ROWS, :]
                    rr.append((above - below) * radial_scale)
                    later = sm[c, i + 2, low : low + ROWS, :]
                    sooner = sm[c, i, low : low + ROWS, :]
                    ar.append((later - sooner) * az_scale)
                    right = jnp.where(is_end, here[c], pltpu.roll(here[c], lanes - 1, 1))
                    left = jnp.where(is_start, here[c], pltpu.roll(here[c], 1, 1))
                    xr.append((right - left) * axial_scale)
                ab = (ar[0] - here[1]) * inv_radius
                bb = (ar[1] + here[0]) * inv_radius
                cb = ar[2] * inv_radius
                diagonal = rr[0] * rr[0] + bb * bb + xr[2] * xr[2]
                cross = ab * rr[1] + xr[0] * rr[2] + xr[1] * cb
                q_out[i, b * ROWS : (b + 1) * ROWS, :] = -0.5 * (diagonal + 2.0 * cross)
                return carry

            lax.fori_loop(0, cells, row_of, 0, unroll=2)

    def put_pressure(c):
        pressure_next(c).wait_recv()
        for e in range(joint):
            k = (c - main) * joint + e
            stage[e] = text[4 * blocks + k]
            mean_out[4, :, radial(k), :] = stage[e, pl.ds(BACK - off_own, cells)] * (1.0 / BLADES)

    hops = BLADES - 1

    @pl.loop(0, chunks + SKEW * hops + LAG)
    def _(s):
        k = s // SPLIT

        @pl.when(jnp.logical_and(s < main, s % SPLIT == 0))
        def _():
            make_carried(k)

            @pl.when(k < blocks - 1)
            def _():
                ahead_density(k + 1).start()
                ahead_flow(k + 1).start()

        @pl.when(jnp.logical_and(s < main, s % SPLIT == SPLIT - 1))
        def _():
            make_tail(k)
            rim_next(k).start()
            rim_prev(k).start()

        u = s - SKEW * blade
        pl.when(jnp.logical_and(u >= 0, u < chunks))(lambda: go_up(u))
        w = s - SKEW * (hops - blade)
        pl.when(jnp.logical_and(w >= 0, w < chunks))(lambda: go_down(w))
        t = s - SKEW * hops
        pl.when(jnp.logical_and(t >= 0, t < chunks))(lambda: finish(t))
        g = t - LAG

        @pl.when(jnp.logical_and(jnp.logical_and(g >= 0, g < main), g % SPLIT == SPLIT - 1))
        def _():
            smooth_block(g // SPLIT)

        pl.when(g == main - 1)(swirl)
        pl.when(g >= main)(lambda: put_pressure(g))

    @pl.loop(0, blocks)
    def _(k):
        ahead_density(k).wait_send()
        ahead_flow(k).wait_send()
        sums_next(k).wait_send()
        sums_prev(k).wait_send()
        rim_next(k).wait_send()
        rim_prev(k).wait_send()

    @pl.loop(0, chunks)
    def _(c):
        pl.when(has_up)(lambda: send_up(psend, c).wait_send())
        pl.when(has_down)(lambda: send_down(ssend, c).wait_send())
        pl.when(c >= main)(lambda: pressure_next(c).wait_send())

    pl.when(has_out)(lambda: edge(1).wait_send())
    pl.when(has_in)(lambda: edge(0).wait_send())


def shards(n_az, n_rad, density, flow_vars, blade_offset, smooth_width):
    cells, rad_cells, axial = density.shape
    blocks = rad_cells // ROWS
    count = 5 * blocks
    chunks = SPLIT * blocks + SPLIT * blocks // 4
    f32 = jnp.float32
    vmem = pl.BlockSpec(memory_space=pltpu.VMEM)
    block = (chunks, 4, cells // SPLIT, ROWS, axial)
    dma = pltpu.SemaphoreType.DMA
    return pl.pallas_call(
        functools.partial(kernel, n_az, n_rad),
        out_shape=(
            jax.ShapeDtypeStruct((5, cells, rad_cells, axial), f32),
            jax.ShapeDtypeStruct((cells, rad_cells, axial), f32),
        ),
        in_specs=[pl.BlockSpec(memory_space=pl.ANY)] * 4,
        out_specs=(vmem, vmem),
        scratch_shapes=[
            pltpu.SMEM((BLADES,), jnp.int32),
            pltpu.VMEM((1, axial), jnp.int32),
            pltpu.VMEM((cells, rad_cells, axial), f32),
            pltpu.VMEM((4, cells, rad_cells, axial), f32),
            pltpu.VMEM((blocks, 5, MAXOFF, ROWS, axial), f32),
            pltpu.VMEM((blocks, 3, RIM, ROWS, axial), f32),
            pltpu.VMEM((blocks, 3, RIM, ROWS, axial), f32),
            pltpu.VMEM(block, f32),
            pltpu.VMEM(block, f32),
            pltpu.VMEM(block, f32),
            pltpu.VMEM(block, f32),
            pltpu.VMEM(block, f32),
            pltpu.VMEM((count, BACK + cells + RIM, ROWS, axial), f32),
            pltpu.VMEM((4, BACK + cells + RIM, ROWS, axial), f32),
            pltpu.VMEM((3, cells + 2 * RIM, ROWS, axial), f32),
            pltpu.VMEM((3, cells + 2, rad_cells + 2 * ROWS, axial), f32),
            pltpu.VMEM((2, 3, cells, axial), f32),
            pltpu.VMEM((2, 3, cells, axial), f32),
            pltpu.VMEM((HW + 1, ROWS, axial), f32),
            dma((2, 2 * blocks)),
            dma((2, 2 * blocks)),
            dma((2, chunks)),
            dma((2, chunks)),
            dma((2, blocks + chunks - SPLIT * blocks)),
            dma((2, blocks)),
            dma((2, 2)),
            dma((4,)),
        ],
        compiler_params=pltpu.CompilerParams(
            collective_id=0, has_side_effects=True, vmem_limit_bytes=56 * 1024 * 1024
        ),
    )(blade_offset, smooth_width.reshape(1, axial), density, flow_vars)


def solution(mesh):
    in_specs = (P("az", "rad", None), P(None, "az", "rad", None), P(), P())
    out_specs = (P(None, "az", "rad", None), P("az", "rad", None))
    body = functools.partial(shards, mesh.shape["az"], mesh.shape["rad"])
    return jax.shard_map(body, mesh=mesh, in_specs=in_specs, out_specs=out_specs, check_vma=False)
```

```python
import functools
import math

import jax
import jax.numpy as jnp
from jax import lax
from jax.experimental import pallas as pl
from jax.experimental.pallas import tpu as pltpu
from jax.sharding import PartitionSpec as P

BLADES = 4
MAXOFF = 4
HW = 4
ROWS = 8
SPLIT = 4
SKEW = 3
LAG = 8
LAST_LAG = 7
RIM = HW + 1
BACK = RIM + MAXOFF
MESH = pl.DeviceIdType.MESH


def kernel(
    n_az,
    n_rad,
    off_hbm,
    width_hbm,
    density_hbm,
    flow_hbm,
    mean_hbm,
    q_hbm,
    mean_out,
    q_out,
    off_ref,
    width_ref,
    density,
    flow,
    ahead,
    vprev,
    vnext,
    cbuf,
    precv,
    psend,
    srecv,
    ssend,
    text,
    stage,
    fl,
    sm,
    edge_s,
    edge_r,
    taps,
    ahead_sem,
    v_sem,
    up_sem,
    down_sem,
    next_sem,
    prev_sem,
    edge_sem,
    load_sem,
    store_sem,
):
    cells, rad_cells = density.shape[0], density.shape[1]
    blocks = rad_cells // ROWS
    main = SPLIT * blocks
    chunks = main + main // 4
    part = cells // SPLIT
    joint = 4 // SPLIT
    group = n_az // BLADES
    place = lax.axis_index("az")
    rad = lax.axis_index("rad")
    blade = place // group
    local = place % group
    first = blade * group
    ring_next = first + (local + 1) % group
    ring_prev = first + (local + group - 1) % group
    cyc_next = (place + 1) % n_az
    cyc_prev = (place + n_az - 1) % n_az
    has_up, has_down = blade < BLADES - 1, blade > 0
    has_out, has_in = rad < n_rad - 1, rad > 0
    up, down = place + group, place - group

    loads = [
        pltpu.make_async_copy(src, dst, load_sem.at[i])
        for i, (src, dst) in enumerate(
            (
                (off_hbm, off_ref),
                (width_hbm, width_ref),
                (density_hbm, density),
                (flow_hbm, flow),
            )
        )
    ]
    for load in loads:
        load.start()

    barrier = pltpu.get_barrier_semaphore()

    def greet(az=None, to_rad=None):
        pl.semaphore_signal(
            barrier,
            inc=1,
            device_id={"az": place if az is None else az, "rad": rad if to_rad is None else to_rad},
            device_id_type=MESH,
        )

    for other in (ring_next, ring_prev, cyc_next, cyc_prev):
        greet(az=other)
    pl.when(has_up)(lambda: greet(az=up))
    pl.when(has_down)(lambda: greet(az=down))
    pl.when(has_out)(lambda: greet(to_rad=rad + 1))
    pl.when(has_in)(lambda: greet(to_rad=rad - 1))

    for load in loads:
        load.wait()

    off_own = off_ref[blade]
    off_before = off_ref[(blade + BLADES - 1) % BLADES]
    off_after = off_ref[(blade + 1) % BLADES]
    off_tail = jnp.where(local == group - 1, off_before, off_own)
    off_low = jnp.where(local == 0, off_before, off_own)
    off_high = jnp.where(local == group - 1, off_after, off_own)

    def phys(k):
        return jnp.where(rad % 2 == 0, blocks - 1 - k, k)

    def radial(k):
        return pl.ds(pl.multiple_of(phys(k) * ROWS, ROWS), ROWS)

    def remote(src, dst, sems, index, az=None, to_rad=None):
        device = {"az": place if az is None else az, "rad": rad if to_rad is None else to_rad}
        return pltpu.make_async_remote_copy(
            src_ref=src,
            dst_ref=dst,
            send_sem=sems.at[0, index],
            recv_sem=sems.at[1, index],
            device_id=device,
            device_id_type=MESH,
        )

    def ahead_density(k):
        return remote(
            density.at[pl.ds(0, MAXOFF), radial(k)], ahead.at[k, 0], ahead_sem, 2 * k, az=ring_prev
        )

    def ahead_flow(k):
        return remote(
            flow.at[:, pl.ds(0, MAXOFF), radial(k)],
            ahead.at[k, pl.ds(1, 4)],
            ahead_sem,
            2 * k + 1,
            az=ring_prev,
        )

    def rim_next(k):
        rows = flow.at[pl.ds(0, 3), pl.ds(cells - RIM, RIM), radial(k)]
        return remote(rows, vprev.at[k], v_sem, 2 * k, az=cyc_next)

    def rim_prev(k):
        rows = flow.at[pl.ds(0, 3), pl.ds(0, RIM), radial(k)]
        return remote(rows, vnext.at[k], v_sem, 2 * k + 1, az=cyc_prev)

    def send_up(src, c):
        return remote(src.at[c], precv.at[c], up_sem, c, az=up)

    def send_down(src, c):
        return remote(src.at[c], srecv.at[c], down_sem, c, az=down)

    def sums_next(k):
        four = pl.ds(4 * k, 4)
        return remote(
            text.at[four, pl.ds(cells, BACK)], text.at[four, pl.ds(0, BACK)], next_sem, k, az=ring_next
        )

    def sums_prev(k):
        four = pl.ds(4 * k, 4)
        return remote(
            text.at[four, pl.ds(BACK, RIM)],
            text.at[four, pl.ds(BACK + cells, RIM)],
            prev_sem,
            k,
            az=ring_prev,
        )

    def pressure_next(c):
        these = pl.ds(4 * blocks + (c - main) * joint, joint)
        return remote(
            text.at[these, pl.ds(BACK + cells - MAXOFF, MAXOFF)],
            text.at[these, pl.ds(BACK - MAXOFF, MAXOFF)],
            next_sem,
            blocks + c - main,
            az=ring_next,
        )

    def edge(side):
        return remote(
            edge_s.at[side], edge_r.at[side], edge_sem, side, to_rad=rad + 1 if side else rad - 1
        )

    def store_fields(k):
        src = mean_out.at[pl.ds(0, 4), :, radial(k)]
        dst = mean_hbm.at[pl.ds(0, 4), :, radial(k)]
        return pltpu.make_async_copy(src, dst, store_sem.at[0, k])

    def store_pressure(k):
        src, dst = mean_out.at[4, :, radial(k)], mean_hbm.at[4, :, radial(k)]
        return pltpu.make_async_copy(src, dst, store_sem.at[1, k])

    def store_q(k):
        src, dst = q_out.at[:, radial(k)], q_hbm.at[:, radial(k)]
        return pltpu.make_async_copy(src, dst, store_sem.at[2, k])

    width = width_ref[...].astype(jnp.float32)
    weights = [
        jnp.where(m <= width_ref[...], jnp.exp((-0.5 * m * m) / (width * width)), 0.0)
        for m in range(HW + 1)
    ]
    whole = weights[0] + 2.0 * sum(weights[1:])
    for m in range(HW + 1):
        taps[m] = jnp.broadcast_to(weights[m] / whole, (ROWS, width.shape[1]))

    greeted = 4
    for flag in (has_up, has_down, has_out, has_in):
        greeted = greeted + jnp.where(flag, 1, 0)
    pl.semaphore_wait(barrier, greeted)

    ahead_density(0).start()
    ahead_flow(0).start()
    sure = cells - MAXOFF

    def pressure_at(k, i):
        unit = SPLIT * k + i // part
        return main + unit // 4, unit % 4

    def make_carried(k):
        js = radial(k)
        for low in range(0, sure, part):
            n = min(part, sure - low)
            rows = pl.ds(off_own + low, n)
            chunk = SPLIT * k + low // part
            rho = density[rows, js, :]
            cbuf[chunk, 0, 0:n] = rho
            for c in range(3):
                cbuf[chunk, 1 + c, 0:n] = rho * flow[c, rows, js, :]
            at, unit = pressure_at(k, low)
            cbuf[at, unit, 0:n] = flow[3, rows, js, :]

    def make_tail(k):
        ahead_density(k).wait_recv()
        ahead_flow(k).wait_recv()
        js = radial(k)
        for i in range(sure, cells):
            row = jnp.minimum(i + off_own, cells - 1)
            mine = jnp.where(i + off_own < cells, 1.0, 0.0)
            rho = density[row, js, :] * mine
            total = [rho] + [rho * flow[c, row, js, :] for c in range(3)]
            total.append(flow[3, row, js, :] * mine)
            for j in range(i - sure + 1):
                theirs = jnp.where(i + off_tail == cells + j, 1.0, 0.0)
                rho = ahead[k, 0, j] * theirs
                terms = [rho] + [rho * ahead[k, 1 + c, j] for c in range(3)]
                terms.append(ahead[k, 4, j] * theirs)
                total = [a + b for a, b in zip(total, terms)]
            for f in range(4):
                cbuf[SPLIT * k + i // part, f, i % part] = total[f]
            at, unit = pressure_at(k, i)
            cbuf[at, unit, i % part] = total[4]

    def go_up(c):
        @pl.when(jnp.logical_not(has_down))
        def _():
            send_up(cbuf, c).start()

        @pl.when(has_down)
        def _():
            send_up(psend, c).wait_recv()

            @pl.when(has_up)
            def _():
                psend[c] = precv[c] + cbuf[c]
                send_up(psend, c).start()

    def go_down(c):
        @pl.when(jnp.logical_not(has_up))
        def _():
            send_down(cbuf, c).start()

        @pl.when(has_up)
        def _():
            send_down(ssend, c).wait_recv()

            @pl.when(has_down)
            def _():
                ssend[c] = srecv[c] + cbuf[c]
                send_down(ssend, c).start()

    def place_sums(c, left, right):
        @pl.when(c < main)
        def _():
            rows = pl.ds(BACK + (c % SPLIT) * part, part)
            text[pl.ds(4 * (c // SPLIT), 4), rows] = left[c] + right[c]

        @pl.when(c >= main)
        def _():
            for e in range(4):
                slot = 4 * blocks + (c - main) * joint + e // SPLIT
                low = BACK + (e % SPLIT) * part
                text[slot, low : low + part] = left[c, e] + right[c, e]

    def finish(c):
        pl.when(jnp.logical_not(has_down))(lambda: place_sums(c, cbuf, srecv))
        pl.when(jnp.logical_not(has_up))(lambda: place_sums(c, cbuf, precv))
        pl.when(jnp.logical_and(has_up, has_down))(lambda: place_sums(c, psend, srecv))

        @pl.when(jnp.logical_and(c < main, c % SPLIT == SPLIT - 1))
        def _():
            sums_next(c // SPLIT).start()
            sums_prev(c // SPLIT).start()

        @pl.when(c >= main)
        def _():
            pressure_next(c).start()

    def smooth_block(k):
        sums_next(k).wait_recv()
        sums_prev(k).wait_recv()
        rim_next(k).wait_recv()
        rim_prev(k).wait_recv()
        js = radial(k)
        for f in range(4):
            stage[f] = text[4 * k + f]
        for at, count, off, source in (
            (0, RIM, off_low, vprev),
            (RIM, cells, off_own, flow),
            (RIM + cells, RIM, off_high, vnext),
        ):
            rows = pl.ds(at + MAXOFF - off, count)
            rho = stage[0, rows]
            inverse = 1.0 / rho
            if source is flow:
                mean_out[0, :, js, :] = rho * (1.0 / BLADES)
            for c in range(3):
                mean = stage[1 + c, rows] * inverse
                if source is flow:
                    mean_out[1 + c, :, js, :] = mean
                here = source[c, :, js, :] if source is flow else source[k, c]
                fl[c, at : at + count] = here - mean
        store_fields(k).start()
        span = cells + 2
        js = pl.ds(pl.multiple_of(ROWS + phys(k) * ROWS, ROWS), ROWS)
        for c in range(3):
            total = taps[0] * fl[c, HW : HW + span]
            for m in range(1, HW + 1):
                total = total + taps[m] * (
                    fl[c, HW - m : HW - m + span] + fl[c, HW + m : HW + m + span]
                )
            sm[c, :, js, :] = total

        @pl.when(jnp.logical_and(has_out, phys(k) == blocks - 1))
        def _():
            for c in range(3):
                edge_s[1, c] = sm[c, 1 : cells + 1, ROWS + rad_cells - 1, :]
            edge(1).start()

        @pl.when(jnp.logical_and(has_in, phys(k) == 0))
        def _():
            for c in range(3):
                edge_s[0, c] = sm[c, 1 : cells + 1, ROWS, :]
            edge(0).start()

    def place_edge(side, have, at, own):
        mid = slice(1, cells + 1)

        @pl.when(have)
        def _():
            edge(side).wait_recv()
            for c in range(3):
                sm[c, mid, at, :] = edge_r[side, c]

        @pl.when(jnp.logical_not(have))
        def _():
            for c in range(3):
                sm[c, mid, at, :] = sm[c, mid, own, :]

    def swirl(k):
        b = phys(k)

        @pl.when(b == blocks - 1)
        def _():
            place_edge(0, has_out, ROWS + rad_cells, ROWS + rad_cells - 1)

        @pl.when(b == 0)
        def _():
            place_edge(1, has_in, ROWS - 1, ROWS)

        shape = (ROWS, density.shape[2])
        lanes = shape[1]
        lane = lax.broadcasted_iota(jnp.int32, shape, 1)
        line = lax.broadcasted_iota(jnp.int32, shape, 0)
        is_end = lane == lanes - 1
        is_start = lane == 0
        axial_scale = jnp.where(jnp.logical_or(is_end, is_start), 1.0, 0.5)
        az_scale = n_az * cells / (4.0 * math.pi)
        rows = rad * rad_cells + b * ROWS + line
        ends = jnp.logical_or(rows == 0, rows == n_rad * rad_cells - 1)
        radial_scale = jnp.where(ends, 1.0, 0.5)
        inv_radius = 1.0 / (n_rad * rad_cells / 2 + rows.astype(jnp.float32) + 0.5)
        inner, outer, middle = (
            pl.ds(pl.multiple_of((b + i) * ROWS, ROWS), ROWS) for i in (0, 2, 1)
        )
        is_top, is_bottom = line == ROWS - 1, line == 0

        def row_of(i, carry):
            here = [sm[c, i + 1, middle, :] for c in range(3)]
            rr, ar, xr = [], [], []
            for c in range(3):
                above = jnp.where(
                    is_top,
                    pltpu.roll(sm[c, i + 1, outer, :], ROWS - 1, 0),
                    pltpu.roll(here[c], ROWS - 1, 0),
                )
                below = jnp.where(
                    is_bottom,
                    pltpu.roll(sm[c, i + 1, inner, :], 1, 0),
                    pltpu.roll(here[c], 1, 0),
                )
                rr.append((above - below) * radial_scale)
                later = sm[c, i + 2, middle, :]
                sooner = sm[c, i, middle, :]
                ar.append((later - sooner) * az_scale)
                right = jnp.where(is_end, here[c], pltpu.roll(here[c], lanes - 1, 1))
                left = jnp.where(is_start, here[c], pltpu.roll(here[c], 1, 1))
                xr.append((right - left) * axial_scale)
            ab = (ar[0] - here[1]) * inv_radius
            bb = (ar[1] + here[0]) * inv_radius
            cb = ar[2] * inv_radius
            diagonal = rr[0] * rr[0] + bb * bb + xr[2] * xr[2]
            cross = ab * rr[1] + xr[0] * rr[2] + xr[1] * cb
            q_out[i, radial(k), :] = -0.5 * (diagonal + 2.0 * cross)
            return carry

        lax.fori_loop(0, cells, row_of, 0, unroll=4)
        store_q(k).start()

    def put_pressure(c):
        pressure_next(c).wait_recv()
        for e in range(joint):
            k = (c - main) * joint + e
            stage[e] = text[4 * blocks + k]
            mean_out[4, :, radial(k), :] = stage[e, pl.ds(BACK - off_own, cells)] * (1.0 / BLADES)
            store_pressure(k).start()

    hops = BLADES - 1

    @pl.loop(0, chunks + SKEW * hops + LAG)
    def _(s):
        k = s // SPLIT

        @pl.when(jnp.logical_and(s < main, s % SPLIT == 0))
        def _():
            make_carried(k)

            @pl.when(k < blocks - 1)
            def _():
                ahead_density(k + 1).start()
                ahead_flow(k + 1).start()

        @pl.when(jnp.logical_and(s < main, s % SPLIT == SPLIT - 1))
        def _():
            make_tail(k)
            rim_next(k).start()
            rim_prev(k).start()

        u = s - SKEW * blade
        pl.when(jnp.logical_and(u >= 0, u < chunks))(lambda: go_up(u))
        w = s - SKEW * (hops - blade)
        pl.when(jnp.logical_and(w >= 0, w < chunks))(lambda: go_down(w))
        t = s - SKEW * hops
        pl.when(jnp.logical_and(t >= 0, t < chunks))(lambda: finish(t))
        g = t - LAG

        early = jnp.logical_and(g >= 0, g < main - SPLIT)
        due = jnp.logical_and(early, g % SPLIT == SPLIT - 1)
        last = t == main - 1 + LAST_LAG

        @pl.when(jnp.logical_or(due, last))
        def _():
            k = jnp.where(last, blocks - 1, g // SPLIT)
            smooth_block(k)
            pl.when(k > 0)(lambda: swirl(k - 1))

        pl.when(last)(lambda: swirl(blocks - 1))
        pl.when(g >= main)(lambda: put_pressure(g))

    @pl.loop(0, blocks)
    def _(k):
        ahead_density(k).wait_send()
        ahead_flow(k).wait_send()
        sums_next(k).wait_send()
        sums_prev(k).wait_send()
        rim_next(k).wait_send()
        rim_prev(k).wait_send()
        store_fields(k).wait()
        store_pressure(k).wait()
        store_q(k).wait()

    @pl.loop(0, chunks)
    def _(c):
        pl.when(has_up)(lambda: send_up(psend, c).wait_send())
        pl.when(has_down)(lambda: send_down(ssend, c).wait_send())
        pl.when(c >= main)(lambda: pressure_next(c).wait_send())

    pl.when(has_out)(lambda: edge(1).wait_send())
    pl.when(has_in)(lambda: edge(0).wait_send())


def shards(n_az, n_rad, density, flow_vars, blade_offset, smooth_width):
    cells, rad_cells, axial = density.shape
    blocks = rad_cells // ROWS
    count = 5 * blocks
    chunks = SPLIT * blocks + SPLIT * blocks // 4
    f32 = jnp.float32
    block = (chunks, 4, cells // SPLIT, ROWS, axial)
    dma = pltpu.SemaphoreType.DMA
    return pl.pallas_call(
        functools.partial(kernel, n_az, n_rad),
        out_shape=(
            jax.ShapeDtypeStruct((5, cells, rad_cells, axial), f32),
            jax.ShapeDtypeStruct((cells, rad_cells, axial), f32),
        ),
        in_specs=[pl.BlockSpec(memory_space=pl.ANY)] * 4,
        out_specs=(pl.BlockSpec(memory_space=pl.ANY),) * 2,
        scratch_shapes=[
            pltpu.VMEM((5, cells, rad_cells, axial), f32),
            pltpu.VMEM((cells, rad_cells, axial), f32),
            pltpu.SMEM((BLADES,), jnp.int32),
            pltpu.VMEM((1, axial), jnp.int32),
            pltpu.VMEM((cells, rad_cells, axial), f32),
            pltpu.VMEM((4, cells, rad_cells, axial), f32),
            pltpu.VMEM((blocks, 5, MAXOFF, ROWS, axial), f32),
            pltpu.VMEM((blocks, 3, RIM, ROWS, axial), f32),
            pltpu.VMEM((blocks, 3, RIM, ROWS, axial), f32),
            pltpu.VMEM(block, f32),
            pltpu.VMEM(block, f32),
            pltpu.VMEM(block, f32),
            pltpu.VMEM(block, f32),
            pltpu.VMEM(block, f32),
            pltpu.VMEM((count, BACK + cells + RIM, ROWS, axial), f32),
            pltpu.VMEM((4, BACK + cells + RIM, ROWS, axial), f32),
            pltpu.VMEM((3, cells + 2 * RIM, ROWS, axial), f32),
            pltpu.VMEM((3, cells + 2, rad_cells + 2 * ROWS, axial), f32),
            pltpu.VMEM((2, 3, cells, axial), f32),
            pltpu.VMEM((2, 3, cells, axial), f32),
            pltpu.VMEM((HW + 1, ROWS, axial), f32),
            dma((2, 2 * blocks)),
            dma((2, 2 * blocks)),
            dma((2, chunks)),
            dma((2, chunks)),
            dma((2, blocks + chunks - SPLIT * blocks)),
            dma((2, blocks)),
            dma((2, 2)),
            dma((4,)),
            dma((3, blocks)),
        ],
        compiler_params=pltpu.CompilerParams(
            collective_id=0, has_side_effects=True, vmem_limit_bytes=56 * 1024 * 1024
        ),
    )(blade_offset, smooth_width.reshape(1, axial), density, flow_vars)


def solution(mesh):
    in_specs = (P("az", "rad", None), P(None, "az", "rad", None), P(), P())
    out_specs = (P(None, "az", "rad", None), P("az", "rad", None))
    body = functools.partial(shards, mesh.shape["az"], mesh.shape["rad"])
    return jax.shard_map(body, mesh=mesh, in_specs=in_specs, out_specs=out_specs, check_vma=False)
```
